32 devices in a mesh: gx: 4 (over y, core), gy: 8 (over z, x).
Axes of the slice: x: 2, y: 2, z: 4, core: 2. Of those that a mesh axis runs over, the one named last changes fastest.
Arguments:
- right_side: float32 [2, 16, 64, 1024], P(None, None, 'gx', 'gy'), may hold values from -12 to 12
- classes: int32 [16, 64, 1024], P(None, 'gx', 'gy'), may hold values from 0 to 15
- sea_mask: int32 [16, 64, 1024], P(None, 'gx', 'gy'), may hold values from 0 to 1, as said below
- kappa_table: float32 [16], replicated, may hold values from 0.002 to 0.2
- cross_table: float32 [16], replicated, may hold values from 0.5 to 4
- vertical_table: float32 [16], replicated, may hold values from 0.05 to 0.5
Outputs:
- solution_field: float32 [2, 16, 64, 1024], P(None, None, 'gx', 'gy')
- residual: float32 [2, 16, 64, 1024], P(None, None, 'gx', 'gy')
The draws below stay inside these ranges and needn't reach their ends.
Inputs may be any that keep to these rules, and one draw needn't show every extreme that they name: `sea_mask`: land cells (value 0) occur only where both horizontal indices of the cell are even.
All inputs are finite; a program needn't handle non-finite values.
Results may differ from the reference program's by a relative error of at most 0.0055.
Values sent between devices are 32-bit elements; how exact they have to be, the bound alone decides.
A program may use at most 128 MiB of HBM per device.

```python
import math
import jax
import jax.numpy as jnp
from jax import lax

NZ = 16
LEVELS = 3
CLASSES = 16
RHS = 2
NX = 64
NY = 1024


def draw_right_side(key, part):
    key = jax.random.fold_in(key, 11)
    across = jnp.arange(NX, dtype=jnp.float32) / NX
    rising = (1.0 + 2.0 * across)[None, None, :, None]
    values = jnp.clip(jax.random.normal(key, (RHS, NZ, NX, NY), jnp.float32), -4.0, 4.0)
    return values * rising


def draw_sea_mask(key, part):
    key = jax.random.fold_in(key, 23)
    candidate = jax.random.randint(key, (NZ, NX, NY), 0, 5) < 3
    even_first = (jnp.arange(NX) % 2 == 0)[None, :, None]
    even_second = (jnp.arange(NY) % 2 == 0)[None, None, :]
    land = candidate & even_first & even_second
    return jnp.where(land, 0, 1).astype(jnp.int32)


def plant(drawn, key, least, high):
    longest = drawn.shape.index(max(drawn.shape))
    spots = []
    for shift in (0, 1):
        where = [jax.random.randint(jax.random.fold_in(key, axis), (), 0, length) for axis, length in enumerate(drawn.shape)]
        where[longest] = (where[longest] + shift) % drawn.shape[longest]
        spots.append(tuple(where))
    return drawn.at[spots[0]].set(least).at[spots[1]].set(high)


def setup_inputs(seed: int = 0) -> dict:
    key_of = jax.random.split(jax.random.key(seed), 7)
    right_side = draw_right_side(jax.random.fold_in(key_of[6], 71), 0)
    classes = plant(jax.random.randint(key_of[1], (NZ, NX, NY), 0, CLASSES), jax.random.fold_in(key_of[1], 1), 0, CLASSES - 1).astype(jnp.int32)
    sea_mask = draw_sea_mask(jax.random.fold_in(key_of[6], 71), 0)
    kappa_table = jnp.clip(jnp.exp(jax.random.uniform(key_of[3], (CLASSES,), jnp.float32, math.log(0.002), math.log(0.2))), 0.002, 0.2)
    cross_table = jnp.clip(jnp.exp(jax.random.uniform(key_of[4], (CLASSES,), jnp.float32, math.log(0.5), math.log(4.0))), 0.5, 4.0)
    vertical_table = jnp.clip(jnp.exp(jax.random.uniform(key_of[5], (CLASSES,), jnp.float32, math.log(0.05), math.log(0.5))), 0.05, 0.5)
    return {"right_side": right_side, "classes": classes, "sea_mask": sea_mask, "kappa_table": kappa_table, "cross_table": cross_table, "vertical_table": vertical_table}


def cheb_weights(degree, lower_end, upper_end):
    middle = 0.5 * (upper_end + lower_end)
    radius = 0.5 * (upper_end - lower_end)
    return [1.0 / (middle + radius * math.cos(math.pi * (2 * index_k + 1) / (2 * degree))) for index_k in range(degree)]

def look_up(classes, values_table):
    result = jnp.zeros(classes.shape, jnp.float32)
    for entry in range(values_table.shape[0]):
        result = jnp.where(classes == entry, values_table[entry], result)
    return result

def coarsen_sum(vector):
    shape = vector.shape
    blocks = vector.reshape(shape[:-3] + (shape[-3] // 2, 2, shape[-2] // 2, 2, shape[-1] // 2, 2))
    return lax.optimization_barrier(jnp.sum(blocks, axis=(-5, -3, -1)))

def coarsen_mean(vector):
    return 0.125 * coarsen_sum(vector)

def spread_up(vector):
    return jnp.repeat(jnp.repeat(jnp.repeat(vector, 2, axis=-3), 2, axis=-2), 2, axis=-1)

def build_coeffs(padded_w, vertical, mass_term, factor):
    face_x = factor * jnp.sqrt(padded_w[:, :-1, 1:-1] * padded_w[:, 1:, 1:-1])
    face_y = factor * jnp.sqrt(padded_w[:, 1:-1, :-1] * padded_w[:, 1:-1, 1:])
    face_z = jnp.pad(factor * jnp.sqrt(vertical[:-1] * vertical[1:]), ((1, 1), (0, 0), (0, 0)))
    diagonal = mass_term + face_x[:, :-1] + face_x[:, 1:] + face_y[:, :, :-1] + face_y[:, :, 1:] + face_z[:-1] + face_z[1:]
    return (face_x, face_y, face_z, diagonal)

def apply_operator(vector, coeffs, padded):
    face_x, face_y, face_z, diagonal = coeffs
    padded_z = jnp.pad(vector, ((0, 0), (1, 1), (0, 0), (0, 0)))
    neighbours = face_x[:, :-1] * padded[:, :, :-2, 1:-1] + face_x[:, 1:] * padded[:, :, 2:, 1:-1]
    neighbours = neighbours + face_y[:, :, :-1] * padded[:, :, 1:-1, :-2] + face_y[:, :, 1:] * padded[:, :, 1:-1, 2:]
    neighbours = neighbours + face_z[:-1] * padded_z[:, :-2] + face_z[1:] * padded_z[:, 2:]
    return diagonal * vector - neighbours

def smooth_pass(approx, source, coeffs, weights, operator):
    for step_index, weight in enumerate(weights):
        if approx is None:
            approx = weight * source / coeffs[3]
        else:
            approx = approx + weight * (source - operator(approx)) / coeffs[3]
    return approx

def pad_sides(vector):
    return jnp.pad(vector, ((0, 0), (0, 0), (1, 1), (1, 1)))

def cycle_down(source, coeff_list, tier_index):
    coeffs = coeff_list[tier_index]

    def operator(vector):
        return apply_operator(vector, coeffs, pad_sides(vector))
    if tier_index == len(coeff_list) - 1:
        return smooth_pass(None, source, coeffs, cheb_weights(4, 0.1, 2.0), operator)
    smooth_weights = cheb_weights(2, 0.3, 2.0)
    approx = smooth_pass(None, source, coeffs, smooth_weights, operator)
    defect = source - operator(approx)
    approx = approx + spread_up(cycle_down(coarsen_sum(defect), coeff_list, tier_index + 1))
    return smooth_pass(approx, source, coeffs, smooth_weights, operator)

def reference(right_side, classes, sea_mask, kappa_table, cross_table, vertical_table):
    sea = sea_mask.astype(jnp.float32)
    crosswise = look_up(classes, cross_table) * sea
    vertical = look_up(classes, vertical_table) * sea
    mass_term = look_up(classes, kappa_table) * sea + (1.0 - sea)
    coeff_list = []
    factor = 1.0
    for tier_index in range(LEVELS):
        padded_w = jnp.pad(crosswise, ((0, 0), (1, 1), (1, 1)))
        coeff_list.append(build_coeffs(padded_w, vertical, mass_term, factor))
        if tier_index < LEVELS - 1:
            crosswise = coarsen_mean(crosswise)
            vertical = coarsen_mean(vertical)
            mass_term = coarsen_sum(mass_term)
            factor = 4.0

    def fine_operator(vector):
        return apply_operator(vector, coeff_list[0], pad_sides(vector))
    direction = cycle_down(cycle_down(right_side, coeff_list, 0), coeff_list, 0)
    image = fine_operator(fine_operator(direction))
    step_length = lax.optimization_barrier(jnp.sum(right_side * direction, axis=(1, 2, 3))) / lax.optimization_barrier(jnp.sum(direction * image, axis=(1, 2, 3)))
    step_length = step_length[:, None, None, None]
    return (step_length * direction, right_side - step_length * image)
```

```python
import functools
import math

import jax
import jax.numpy as jnp
from jax import lax
from jax.experimental import pallas as pl
from jax.experimental.pallas import tpu as pltpu
from jax.sharding import PartitionSpec as P

MESH = pl.DeviceIdType.MESH
ROWS, LANES = 16, 128
WIDE = 2 * LANES
WAYS = ((-1, 0), (1, 0), (0, -1), (0, 1), (-1, -1), (1, -1), (-1, 1), (1, 1))


def cheb_weights(degree, lower_end, upper_end):
    middle = 0.5 * (upper_end + lower_end)
    radius = 0.5 * (upper_end - lower_end)
    return [
        1.0 / (middle + radius * math.cos(math.pi * (2 * index_k + 1) / (2 * degree)))
        for index_k in range(degree)
    ]


def turn(value, shift, axis):
    size = value.shape[axis]
    shift = shift % size
    return value if shift == 0 else pltpu.roll(value, shift, axis)


def pair_sum(value, step):
    for axis in (value.ndim - 2, value.ndim - 1):
        place = lax.broadcasted_iota(jnp.int32, value.shape, axis)
        first = (place // step) % 2 == 0
        value = value + jnp.where(first, turn(value, -step, axis), turn(value, step, axis))
    return value


def loop(count, body):
    def run(index, carry):
        body(index)
        return carry

    lax.fori_loop(0, count, run, 0)


class Level:
    def __init__(self, refs, depth, step, factor):
        self.w, self.u, self.k, self.fxm, self.fxp, self.fym, self.fyp, self.fz, self.d, self.inv = refs
        self.depth, self.step, self.factor = depth, step, factor

    def build(self, diagonal_known=False):
        step, factor = self.step, self.factor

        def body(z):
            w = self.w[z + 1]
            fxp = factor * jnp.sqrt(w * turn(w, -step, 0))
            fyp = factor * jnp.sqrt(w * turn(w, -step, 1))
            fxm = turn(fxp, step, 0)
            fym = turn(fyp, step, 1)
            fzm = factor * jnp.sqrt(self.u[z] * self.u[z + 1])
            fzp = factor * jnp.sqrt(self.u[z + 1] * self.u[z + 2])
            d = self.k[z + 1]
            if not diagonal_known:
                d = d + fxm + fxp + fym + fyp + fzm + fzp
            self.fxm[z], self.fxp[z], self.fym[z], self.fyp[z] = fxm, fxp, fym, fyp
            self.fz[z] = fzm
            self.fz[z + 1] = fzp
            self.d[z] = d
            self.inv[z] = jnp.where(d > 0.0, 1.0 / jnp.where(d > 0.0, d, 1.0), 0.0)

        loop(self.depth, body)

    def operator(self, v, z):
        x = v[:, z + 1]
        step = self.step
        total = self.fxm[z] * turn(x, step, 1) + self.fxp[z] * turn(x, -step, 1)
        total = total + self.fym[z] * turn(x, step, 2) + self.fyp[z] * turn(x, -step, 2)
        total = total + self.fz[z] * v[:, z] + self.fz[z + 1] * v[:, z + 2]
        return self.d[z] * x - total

    def start(self, out, r, weight):
        def body(z):
            out[:, z + 1] = weight * r[:, z + 1] * self.inv[z]

        loop(self.depth, body)

    def smooth(self, out, v, r, weight):
        def body(z):
            out[:, z + 1] = v[:, z + 1] + weight * (r[:, z + 1] - self.operator(v, z)) * self.inv[z]

        loop(self.depth, body)


class Exchange:
    def __init__(self, refs, send_sem, recv_sem, row, width, depth):
        self.left, self.right, self.rows_in, self.from_right, self.from_left = refs
        self.send_sem, self.recv_sem, self.row = send_sem, recv_sem, row
        self.width, self.depth = width, depth

    def clear(self):
        for ref in (self.rows_in, self.from_right, self.from_left):
            ref[...] = jnp.zeros(ref.shape, jnp.float32)

    def pack(self, source):
        width, groups = self.width, LANES // self.width
        shape = self.left.shape
        group = lax.broadcasted_iota(jnp.int32, shape, 2) // width
        left = jnp.zeros(shape, jnp.float32)
        right = jnp.zeros(shape, jnp.float32)
        for z in range(self.depth):
            moved = turn(source[:, z], width * z, 2)
            left = jnp.where(group == z, moved, left)
            right = jnp.where(group == (z - 1) % groups, moved, right)
        self.left[...] = left
        self.right[...] = right

    def copies(self, source):
        h = self.width
        low, high = pl.ds(0, h), pl.ds(ROWS - h, h)
        near, far = pl.ds(ROWS, h), pl.ds(ROWS + h, h)
        whole = pl.ds(0, ROWS)
        ends = (
            (source.at[:, :, low], self.rows_in.at[:, :, pl.ds(0, h)]),
            (source.at[:, :, high], self.rows_in.at[:, :, pl.ds(h, h)]),
            (self.left, self.from_right.at[:, whole]),
            (self.right, self.from_left.at[:, whole]),
            (self.left.at[:, low], self.from_right.at[:, near]),
            (self.left.at[:, high], self.from_right.at[:, far]),
            (self.right.at[:, low], self.from_left.at[:, near]),
            (self.right.at[:, high], self.from_left.at[:, far]),
        )
        gx, gy = lax.axis_index("gx"), lax.axis_index("gy")
        nx, ny = lax.axis_size("gx"), lax.axis_size("gy")
        for way, ((dx, dy), (src, dst)) in enumerate(zip(WAYS, ends)):
            copy = pltpu.make_async_remote_copy(
                src_ref=src,
                dst_ref=dst,
                send_sem=self.send_sem.at[self.row, way],
                recv_sem=self.recv_sem.at[self.row, way],
                device_id=(lax.rem(gx + dx + nx, nx), lax.rem(gy + dy + ny, ny)),
                device_id_type=MESH,
            )
            yield copy, exists(gx, nx, dx) & exists(gy, ny, dy), exists(gx, nx, -dx) & exists(gy, ny, -dy)

    def begin(self, source):
        self.pack(source)
        for copy, sends, _ in self.copies(source):
            pl.when(sends)(copy.start)

    def finish(self, source):
        for copy, sends, receives in self.copies(source):
            pl.when(sends)(copy.wait_send)
            pl.when(receives)(copy.wait_recv)

    def unpack(self, out, source, count):
        h = self.width
        lane = lax.broadcasted_iota(jnp.int32, self.from_right.shape, 2)
        from_right, from_left = self.from_right[...], self.from_left[...]
        for z in range(self.depth):
            side = jnp.where(
                lane < h,
                turn(from_right, -h * z, 2),
                jnp.where(lane >= LANES - h, turn(from_left, -h * z, 2), 0.0),
            )
            for item in range(count):
                target = out[item] if isinstance(out, tuple) else out.at[item]
                if source is not None:
                    target[z + 1, 0:ROWS, 0:LANES] = source[item, z]
                target[z + 1, ROWS : ROWS + 2 * h, 0:LANES] = self.rows_in[item, z]
                target[z + 1, :, LANES:WIDE] = side[item]


def exists(index, count, step):
    if step < 0:
        return index > 0
    if step > 0:
        return index < count - 1
    return index >= 0


def greet():
    gx, gy = lax.axis_index("gx"), lax.axis_index("gy")
    nx, ny = lax.axis_size("gx"), lax.axis_size("gy")
    barrier = pltpu.get_barrier_semaphore()
    for step in range(1, nx):
        pl.semaphore_signal(barrier, inc=1, device_id=(lax.rem(gx + step, nx), gy), device_id_type=MESH)
    for step in range(1, ny):
        pl.semaphore_signal(barrier, inc=1, device_id=(gx, lax.rem(gy + step, ny)), device_id_type=MESH)
    for dx, dy in WAYS[4:]:
        there = (lax.rem(gx + dx + nx, nx), lax.rem(gy + dy + ny, ny))

        @pl.when(exists(gx, nx, dx) & exists(gy, ny, dy))
        def _():
            pl.semaphore_signal(barrier, inc=1, device_id=there, device_id_type=MESH)

    beside_x = (gx > 0).astype(jnp.int32) + (gx < nx - 1).astype(jnp.int32)
    beside_y = (gy > 0).astype(jnp.int32) + (gy < ny - 1).astype(jnp.int32)
    pl.semaphore_wait(barrier, nx - 1 + ny - 1 + beside_x * beside_y)


def sum_over(axis, mine, slots, send_sem, recv_sem):
    count = lax.axis_size(axis)
    me = lax.axis_index(axis)
    copies = []
    for step in range(1, count):
        copy = pltpu.make_async_remote_copy(
            src_ref=mine,
            dst_ref=slots.at[step - 1],
            send_sem=send_sem.at[step - 1],
            recv_sem=recv_sem.at[step - 1],
            device_id={axis: lax.rem(me + step, count)},
            device_id_type=MESH,
        )
        copy.start()
        copies.append(copy)
    total = mine[...]
    for step, copy in enumerate(copies):
        copy.wait()
        total = total + slots[step]
    return total


def kernel(depth, entries, *refs):
    refs = list(refs)

    def take(count):
        got = tuple(refs[:count])
        del refs[:count]
        return got

    right_side, classes, sea_mask, kappa, cross, vertical = take(6)
    direction_out, image_out, alpha_out = take(3)
    level0 = Level(take(10), depth, 1, 1.0)
    level1 = Level(take(10), depth // 2, 2, 4.0)
    level2 = Level(take(10), depth // 4, 4, 4.0)
    inner2 = Level(take(10), depth // 4, 4, 4.0)
    r_first, r_second, xa, xb = take(4)
    r1, ya, yb = take(3)
    r2, za, zb = take(3)
    material, material2, = take(2)
    r2_own = take(2)
    y_own = take(2)
    x_own = take(2)
    names = ("r", "mat", "mat2", "e2a", "e2b", "ya", "yb", "e4a", "e4b")
    boxes = [take(5) for _ in names]
    part_x, part_y, slots_x, slots_y = take(4)
    send_sem, recv_sem, sx_send, sx_recv, sy_send, sy_recv = take(6)
    widths = (8, 8, 16, 16, 16, 8, 8, 8, 8)
    depths = (depth, depth, depth // 4, depth // 4, depth // 4, depth // 2, depth // 2, depth, depth)
    ex = {
        name: Exchange(box, send_sem, recv_sem, row, width, size)
        for row, (name, box, width, size) in enumerate(zip(names, boxes, widths, depths))
    }
    for exchange in ex.values():
        exchange.clear()
    greet()

    ex["r"].begin(right_side)

    def look_up(z):
        cls = classes[z]
        sea = sea_mask[z].astype(jnp.float32)
        w = jnp.zeros(cls.shape, jnp.float32)
        u, k = w, w
        for entry in range(entries):
            here = cls == entry
            w = jnp.where(here, cross[entry], w)
            u = jnp.where(here, vertical[entry], u)
            k = jnp.where(here, kappa[entry], k)
        material[0, z] = w * sea
        material[1, z] = u * sea
        material[2, z] = k * sea + (1.0 - sea)

    loop(depth, look_up)
    ex["mat"].begin(material)
    for ref in (r_first, r_second, xa, xb, r1, ya, yb, r2, za, zb):
        last = ref.shape[1] - 1
        ref[:, 0] = jnp.zeros(ref.shape[:1] + ref.shape[2:], jnp.float32)
        ref[:, last] = jnp.zeros(ref.shape[:1] + ref.shape[2:], jnp.float32)
    for level in (level0, level1, level2, inner2):
        level.u[0] = jnp.zeros(level.u.shape[1:], jnp.float32)
        level.u[level.depth + 1] = jnp.zeros(level.u.shape[1:], jnp.float32)
    ex["r"].finish(right_side)
    ex["r"].unpack(r_first, right_side, 2)
    ex["mat"].finish(material)
    ex["mat"].unpack((level0.w, level0.u, level0.k), material, 3)

    def coarsen_material(fine, coarse, step):
        def body(z):
            for src, dst, factor in (
                (fine.w, coarse.w, 0.125),
                (fine.u, coarse.u, 0.125),
                (fine.k, coarse.k, 1.0),
            ):
                dst[z + 1] = factor * pair_sum(src[2 * z + 1] + src[2 * z + 2], step)

        loop(coarse.depth, body)

    coarsen_material(level0, level1, 1)
    coarsen_material(level1, inner2, 2)
    inner2.build()

    def own_material2(z):
        material2[0, z] = inner2.w[z + 1, 0:ROWS, 0:LANES]
        material2[1, z] = inner2.u[z + 1, 0:ROWS, 0:LANES]
        material2[2, z] = inner2.d[z, 0:ROWS, 0:LANES]

    loop(level2.depth, own_material2)
    ex["mat2"].begin(material2)
    level0.build()
    level1.build()

    fine_w = cheb_weights(2, 0.3, 2.0)
    coarse_w = cheb_weights(4, 0.1, 2.0)

    def cycle(r, out, turn_no):
        level0.start(xa, r, fine_w[0])
        level0.smooth(xb, xa, r, fine_w[1])

        def down0(z):
            q = r[:, 2 * z + 1] - level0.operator(xb, 2 * z)
            q = q + (r[:, 2 * z + 2] - level0.operator(xb, 2 * z + 1))
            q = pair_sum(q, 1)
            r1[:, z + 1] = q
            ya[:, z + 1] = fine_w[0] * q * level1.inv[z]

        loop(level1.depth, down0)
        level1.smooth(yb, ya, r1, fine_w[1])
        own2 = r2_own[turn_no]

        def down1(z):
            q = r1[:, 2 * z + 1] - level1.operator(yb, 2 * z)
            q = q + (r1[:, 2 * z + 2] - level1.operator(yb, 2 * z + 1))
            own2[:, z] = pair_sum(q, 2)[:, 0:ROWS, 0:LANES]

        loop(level2.depth, down1)
        e2 = ex[("e2a", "e2b")[turn_no]]
        e2.begin(own2)
        own1 = y_own[turn_no]

        def keep(z):
            own1[:, z] = yb[:, z + 1, 0:ROWS, 0:LANES]

        loop(level1.depth, keep)
        e1 = ex[("ya", "yb")[turn_no]]
        e1.begin(own1)
        if turn_no == 0:
            ex["mat2"].finish(material2)
            ex["mat2"].unpack((level2.w, level2.u, level2.k), material2, 3)
            level2.build(True)
        e2.finish(own2)
        e2.unpack(r2, own2, 2)
        level2.start(za, r2, coarse_w[0])
        level2.smooth(zb, za, r2, coarse_w[1])
        level2.smooth(za, zb, r2, coarse_w[2])
        level2.smooth(zb, za, r2, coarse_w[3])
        e1.finish(own1)
        e1.unpack(yb, None, 2)

        def up1(z):
            add = jnp.concatenate([zb[:, z + 1, 0:24], zb[:, z + 1, 40:48]], axis=1)
            ya[:, 2 * z + 1] = yb[:, 2 * z + 1] + add
            ya[:, 2 * z + 2] = yb[:, 2 * z + 2] + add

        loop(level2.depth, up1)
        level1.smooth(yb, ya, r1, fine_w[0])
        level1.smooth(ya, yb, r1, fine_w[1])
        own = x_own[turn_no]

        def up0(z):
            add = ya[:, z + 1, 0:ROWS, 0:LANES]
            own[:, 2 * z] = xb[:, 2 * z + 1, 0:ROWS, 0:LANES] + add
            own[:, 2 * z + 1] = xb[:, 2 * z + 2, 0:ROWS, 0:LANES] + add

        loop(level1.depth, up0)
        e4 = ex[("e4a", "e4b")[turn_no]]
        e4.begin(own)
        e4.finish(own)
        e4.unpack(xa, own, 2)
        level0.smooth(xb, xa, r, fine_w[0])
        level0.smooth(out, xb, r, fine_w[1])

    cycle(r_first, r_second, 0)
    cycle(r_second, r_first, 1)

    def first_image(z):
        xb[:, z + 1] = level0.operator(r_first, z)

    loop(depth, first_image)

    def second_image(z, sums):
        image = level0.operator(xb, z)[:, 0:ROWS, 0:LANES]
        direction = r_first[:, z + 1, 0:ROWS, 0:LANES]
        direction_out[:, z] = direction
        image_out[:, z] = image
        return sums[0] + right_side[:, z] * direction, sums[1] + direction * image

    zero = jnp.zeros((2, ROWS, LANES), jnp.float32)
    rz, curve = lax.fori_loop(0, depth, second_image, (zero, zero))
    part_x[0:2] = rz[:, 0:8] + rz[:, 8:16]
    part_x[2:4] = curve[:, 0:8] + curve[:, 8:16]
    part_y[...] = sum_over("gx", part_x, slots_x, sx_send, sx_recv)
    total = sum_over("gy", part_y, slots_y, sy_send, sy_recv)
    total = jnp.sum(total, axis=2, keepdims=True)
    total = jnp.sum(total, axis=1, keepdims=True)
    alpha_out[...] = jnp.broadcast_to(total[0:2] / total[2:4], alpha_out.shape)


def shards(right_side, classes, sea_mask, kappa_table, cross_table, vertical_table):
    nx, ny = lax.axis_size("gx"), lax.axis_size("gy")
    depth = classes.shape[0]

    def buf(*shape):
        return pltpu.VMEM(shape, jnp.float32)

    def level(size, rows):
        pad, one, face = buf(size + 2, rows, WIDE), buf(size, rows, WIDE), buf(size + 1, rows, WIDE)
        return [pad, pad, pad, one, one, one, one, face, one, one]

    def box(items, size, width):
        sides = buf(items, ROWS + 2 * width, LANES)
        pack = buf(items, ROWS, LANES)
        return [pack, pack, buf(items, size, 2 * width, LANES), sides, sides]

    d0, d1, d2 = depth, depth // 2, depth // 4
    scratch = level(d0, 32) + level(d1, 32) + level(d2, 48) + level(d2, 32)
    scratch += [buf(2, d0 + 2, 32, WIDE)] * 4
    scratch += [buf(2, d1 + 2, 32, WIDE)] * 3
    scratch += [buf(2, d2 + 2, 48, WIDE)] * 3
    scratch += [buf(3, d0, ROWS, LANES), buf(3, d2, ROWS, LANES)]
    scratch += [buf(2, d2, ROWS, LANES)] * 2 + [buf(2, d1, ROWS, LANES)] * 2 + [buf(2, d0, ROWS, LANES)] * 2
    scratch += box(2, d0, 8) + box(3, d0, 8) + box(3, d2, 16) + box(2, d2, 16) + box(2, d2, 16)
    scratch += box(2, d1, 8) + box(2, d1, 8) + box(2, d0, 8) + box(2, d0, 8)
    scratch += [buf(4, 8, LANES)] * 2 + [buf(nx - 1, 4, 8, LANES), buf(ny - 1, 4, 8, LANES)]
    dma = pltpu.SemaphoreType.DMA
    scratch += [dma((9, 8)), dma((9, 8)), dma((nx - 1,)), dma((nx - 1,)), dma((ny - 1,)), dma((ny - 1,))]
    vmem = pl.BlockSpec(memory_space=pltpu.VMEM)
    smem = pl.BlockSpec(memory_space=pltpu.SMEM)
    field = jax.ShapeDtypeStruct(right_side.shape, jnp.float32)
    direction, image, alpha = pl.pallas_call(
        functools.partial(kernel, depth, kappa_table.shape[0]),
        out_shape=(field, field, jax.ShapeDtypeStruct((2, 8, LANES), jnp.float32)),
        in_specs=[vmem, vmem, vmem, smem, smem, smem],
        out_specs=(vmem, vmem, vmem),
        scratch_shapes=scratch,
        compiler_params=pltpu.CompilerParams(
            collective_id=0, has_side_effects=True, vmem_limit_bytes=48 * 1024 * 1024
        ),
    )(right_side, classes, sea_mask, kappa_table, cross_table, vertical_table)
    alpha = alpha[:, 0:1, 0:1, None]
    return alpha * direction, right_side - alpha * image


def solution(mesh):
    return jax.shard_map(
        shards,
        mesh=mesh,
        in_specs=(
            P(None, None, "gx", "gy"),
            P(None, "gx", "gy"),
            P(None, "gx", "gy"),
            P(),
            P(),
            P(),
        ),
        out_specs=(P(None, None, "gx", "gy"), P(None, None, "gx", "gy")),
        check_vma=False,
    )
```

```python
import functools
import math

import jax
import jax.numpy as jnp
from jax import lax
from jax.experimental import pallas as pl
from jax.experimental.pallas import tpu as pltpu
from jax.sharding import PartitionSpec as P

MESH = pl.DeviceIdType.MESH
ROWS, LANES = 16, 128
WIDE = 2 * LANES
WAYS = ((-1, 0), (1, 0), (0, -1), (0, 1), (-1, -1), (1, -1), (-1, 1), (1, 1))


def cheb_weights(degree, lower_end, upper_end):
    middle = 0.5 * (upper_end + lower_end)
    radius = 0.5 * (upper_end - lower_end)
    return [
        1.0 / (middle + radius * math.cos(math.pi * (2 * index_k + 1) / (2 * degree)))
        for index_k in range(degree)
    ]


def turn(value, shift, axis):
    size = value.shape[axis]
    shift = shift % size
    return value if shift == 0 else pltpu.roll(value, shift, axis)


def pair_sum(value, step):
    for axis in (value.ndim - 2, value.ndim - 1):
        place = lax.broadcasted_iota(jnp.int32, value.shape, axis)
        first = (place // step) % 2 == 0
        value = value + jnp.where(first, turn(value, -step, axis), turn(value, step, axis))
    return value


def loop(count, body):
    def run(index, carry):
        body(index)
        return carry

    lax.fori_loop(0, count, run, 0)


class Level:
    def __init__(self, refs, depth, step, factor):
        self.w, self.u, self.k, self.fxm, self.fxp, self.fym, self.fyp, self.fz, self.d, self.inv = refs
        self.depth, self.step, self.factor = depth, step, factor

    def build(self, diagonal_known=False):
        step, factor = self.step, self.factor

        def body(z):
            w = self.w[z + 1]
            fxp = factor * jnp.sqrt(w * turn(w, -step, 0))
            fyp = factor * jnp.sqrt(w * turn(w, -step, 1))
            fxm = turn(fxp, step, 0)
            fym = turn(fyp, step, 1)
            fzm = factor * jnp.sqrt(self.u[z] * self.u[z + 1])
            fzp = factor * jnp.sqrt(self.u[z + 1] * self.u[z + 2])
            d = self.k[z + 1]
            if not diagonal_known:
                d = d + fxm + fxp + fym + fyp + fzm + fzp
            self.fxm[z], self.fxp[z], self.fym[z], self.fyp[z] = fxm, fxp, fym, fyp
            self.fz[z] = fzm
            self.fz[z + 1] = fzp
            self.d[z] = d
            self.inv[z] = jnp.where(d > 0.0, 1.0 / jnp.where(d > 0.0, d, 1.0), 0.0)

        loop(self.depth, body)

    def operators(self, v, z, count):
        step = self.step
        images = [[None, None] for _ in range(count)]
        faces = [self.fz[z + i] for i in range(count + 1)]
        for item in range(2):
            planes = [v[item, z + i] for i in range(count + 2)]
            for i in range(count):
                x = planes[i + 1]
                total = self.fxm[z + i] * turn(x, step, 0) + self.fxp[z + i] * turn(x, -step, 0)
                total = total + self.fym[z + i] * turn(x, step, 1) + self.fyp[z + i] * turn(x, -step, 1)
                total = total + faces[i] * planes[i] + faces[i + 1] * planes[i + 2]
                images[i][item] = self.d[z + i] * x - total
        return images

    def start(self, out, r, weight):
        def body(pair):
            for i in range(2):
                scale = weight * self.inv[2 * pair + i]
                out[:, 2 * pair + i + 1] = r[:, 2 * pair + i + 1] * scale

        loop(self.depth // 2, body)

    def smooth(self, out, v, r, weight, own_only=False):
        def body(pair):
            z = 2 * pair
            images = self.operators(v, z, 2)
            fresh = []
            for i in range(2):
                scale = weight * self.inv[z + i]
                for item in range(2):
                    defect = r[item, z + i + 1] - images[i][item]
                    fresh.append((item, i, v[item, z + i + 1] + scale * defect))
            for item, i, value in fresh:
                if own_only:
                    out[item, z + i + 1, 0:ROWS, 0:LANES] = value[0:ROWS, 0:LANES]
                else:
                    out[item, z + i + 1] = value

        loop(self.depth // 2, body)

    def defect_sums(self, v, r, pair):
        z = 2 * pair
        images = self.operators(v, z, 2)
        sums = []
        for item in range(2):
            q = (r[item, z + 1] - images[0][item]) + (r[item, z + 2] - images[1][item])
            sums.append(pair_sum(q, self.step))
        return sums


class Exchange:
    def __init__(self, refs, send_sem, recv_sem, row, width, depth):
        self.left, self.right, self.rows_in, self.from_right, self.from_left = refs
        self.send_sem, self.recv_sem, self.row = send_sem, recv_sem, row
        self.width, self.depth = width, depth

    def clear(self):
        for ref in (self.rows_in, self.from_right, self.from_left):
            ref[...] = jnp.zeros(ref.shape, jnp.float32)

    def pack(self, source):
        width, groups = self.width, LANES // self.width
        shape = self.left.shape
        group = lax.broadcasted_iota(jnp.int32, shape, 2) // width
        left = jnp.zeros(shape, jnp.float32)
        right = jnp.zeros(shape, jnp.float32)
        for z in range(self.depth):
            moved = turn(source[:, z], width * z, 2)
            left = jnp.where(group == z, moved, left)
            right = jnp.where(group == (z - 1) % groups, moved, right)
        self.left[...] = left
        self.right[...] = right

    def copies(self, source):
        h = self.width
        low, high = pl.ds(0, h), pl.ds(ROWS - h, h)
        near, far = pl.ds(ROWS, h), pl.ds(ROWS + h, h)
        whole = pl.ds(0, ROWS)
        ends = (
            (source.at[:, :, low], self.rows_in.at[:, :, pl.ds(0, h)]),
            (source.at[:, :, high], self.rows_in.at[:, :, pl.ds(h, h)]),
            (self.left, self.from_right.at[:, whole]),
            (self.right, self.from_left.at[:, whole]),
            (self.left.at[:, low], self.from_right.at[:, near]),
            (self.left.at[:, high], self.from_right.at[:, far]),
            (self.right.at[:, low], self.from_left.at[:, near]),
            (self.right.at[:, high], self.from_left.at[:, far]),
        )
        gx, gy = lax.axis_index("gx"), lax.axis_index("gy")
        nx, ny = lax.axis_size("gx"), lax.axis_size("gy")
        for way, ((dx, dy), (src, dst)) in enumerate(zip(WAYS, ends)):
            copy = pltpu.make_async_remote_copy(
                src_ref=src,
                dst_ref=dst,
                send_sem=self.send_sem.at[self.row, way],
                recv_sem=self.recv_sem.at[self.row, way],
                device_id=(lax.rem(gx + dx + nx, nx), lax.rem(gy + dy + ny, ny)),
                device_id_type=MESH,
            )
            yield copy, exists(gx, nx, dx) & exists(gy, ny, dy), exists(gx, nx, -dx) & exists(gy, ny, -dy)

    def begin(self, source):
        self.pack(source)
        for copy, sends, _ in self.copies(source):
            pl.when(sends)(copy.start)

    def finish(self, source):
        for copy, sends, receives in self.copies(source):
            pl.when(sends)(copy.wait_send)
            pl.when(receives)(copy.wait_recv)

    def unpack(self, out, source, count):
        h = self.width
        lane = lax.broadcasted_iota(jnp.int32, self.from_right.shape, 2)
        from_right, from_left = self.from_right[...], self.from_left[...]
        for z in range(self.depth):
            side = jnp.where(
                lane < h,
                turn(from_right, -h * z, 2),
                jnp.where(lane >= LANES - h, turn(from_left, -h * z, 2), 0.0),
            )
            for item in range(count):
                target = out[item] if isinstance(out, tuple) else out.at[item]
                if source is not None:
                    target[z + 1, 0:ROWS, 0:LANES] = source[item, z]
                target[z + 1, ROWS : ROWS + 2 * h, 0:LANES] = self.rows_in[item, z]
                target[z + 1, :, LANES:WIDE] = side[item]


def exists(index, count, step):
    if step < 0:
        return index > 0
    if step > 0:
        return index < count - 1
    return index >= 0


def greet():
    gx, gy = lax.axis_index("gx"), lax.axis_index("gy")
    nx, ny = lax.axis_size("gx"), lax.axis_size("gy")
    barrier = pltpu.get_barrier_semaphore()
    for step in range(1, nx):
        pl.semaphore_signal(barrier, inc=1, device_id=(lax.rem(gx + step, nx), gy), device_id_type=MESH)
    for step in range(1, ny):
        pl.semaphore_signal(barrier, inc=1, device_id=(gx, lax.rem(gy + step, ny)), device_id_type=MESH)
    for dx, dy in WAYS[4:]:
        there = (lax.rem(gx + dx + nx, nx), lax.rem(gy + dy + ny, ny))

        @pl.when(exists(gx, nx, dx) & exists(gy, ny, dy))
        def _():
            pl.semaphore_signal(barrier, inc=1, device_id=there, device_id_type=MESH)

    beside_x = (gx > 0).astype(jnp.int32) + (gx < nx - 1).astype(jnp.int32)
    beside_y = (gy > 0).astype(jnp.int32) + (gy < ny - 1).astype(jnp.int32)
    pl.semaphore_wait(barrier, nx - 1 + ny - 1 + beside_x * beside_y)


def sum_over(axis, mine, slots, send_sem, recv_sem):
    count = lax.axis_size(axis)
    me = lax.axis_index(axis)
    copies = []
    for step in range(1, count):
        copy = pltpu.make_async_remote_copy(
            src_ref=mine,
            dst_ref=slots.at[step - 1],
            send_sem=send_sem.at[step - 1],
            recv_sem=recv_sem.at[step - 1],
            device_id={axis: lax.rem(me + step, count)},
            device_id_type=MESH,
        )
        copy.start()
        copies.append(copy)
    total = mine[...]
    for step, copy in enumerate(copies):
        copy.wait()
        total = total + slots[step]
    return total


def kernel(depth, entries, *refs):
    refs = list(refs)

    def take(count):
        got = tuple(refs[:count])
        del refs[:count]
        return got

    right_side, classes, sea_mask, kappa, cross, vertical = take(6)
    direction_out, image_out, alpha_out = take(3)
    level0 = Level(take(10), depth, 1, 1.0)
    level1 = Level(take(10), depth // 2, 2, 4.0)
    level2 = Level(take(10), depth // 4, 4, 4.0)
    inner2 = Level(take(10), depth // 4, 4, 4.0)
    r_first, r_second, xa, xb = take(4)
    r1, ya, yb = take(3)
    r2, za, zb = take(3)
    material, material2, = take(2)
    r2_own = take(2)
    y_own = take(2)
    x_own = take(2)
    names = ("r", "mat", "mat2", "e2a", "e2b", "ya", "yb", "e4a", "e4b")
    boxes = [take(5) for _ in names]
    part_x, part_y, slots_x, slots_y = take(4)
    send_sem, recv_sem, sx_send, sx_recv, sy_send, sy_recv = take(6)
    widths = (8, 8, 16, 16, 16, 8, 8, 8, 8)
    depths = (depth, depth, depth // 4, depth // 4, depth // 4, depth // 2, depth // 2, depth, depth)
    ex = {
        name: Exchange(box, send_sem, recv_sem, row, width, size)
        for row, (name, box, width, size) in enumerate(zip(names, boxes, widths, depths))
    }
    for exchange in ex.values():
        exchange.clear()
    greet()

    ex["r"].begin(right_side)

    def look_up(z):
        cls = classes[z]
        sea = sea_mask[z].astype(jnp.float32)
        w = jnp.zeros(cls.shape, jnp.float32)
        u, k = w, w
        for entry in range(entries):
            here = cls == entry
            w = jnp.where(here, cross[entry], w)
            u = jnp.where(here, vertical[entry], u)
            k = jnp.where(here, kappa[entry], k)
        material[0, z] = w * sea
        material[1, z] = u * sea
        material[2, z] = k * sea + (1.0 - sea)

    loop(depth, look_up)
    ex["mat"].begin(material)
    for ref in (r_first, r_second, xa, xb, r1, ya, yb, r2, za, zb):
        last = ref.shape[1] - 1
        ref[:, 0] = jnp.zeros(ref.shape[:1] + ref.shape[2:], jnp.float32)
        ref[:, last] = jnp.zeros(ref.shape[:1] + ref.shape[2:], jnp.float32)
    for level in (level0, level1, level2, inner2):
        level.u[0] = jnp.zeros(level.u.shape[1:], jnp.float32)
        level.u[level.depth + 1] = jnp.zeros(level.u.shape[1:], jnp.float32)
    ex["r"].finish(right_side)
    ex["r"].unpack(r_first, right_side, 2)
    ex["mat"].finish(material)
    ex["mat"].unpack((level0.w, level0.u, level0.k), material, 3)

    def coarsen_material(fine, coarse, step):
        def body(z):
            for src, dst, factor in (
                (fine.w, coarse.w, 0.125),
                (fine.u, coarse.u, 0.125),
                (fine.k, coarse.k, 1.0),
            ):
                dst[z + 1] = factor * pair_sum(src[2 * z + 1] + src[2 * z + 2], step)

        loop(coarse.depth, body)

    coarsen_material(level0, level1, 1)
    coarsen_material(level1, inner2, 2)
    inner2.build()

    def own_material2(z):
        material2[0, z] = inner2.w[z + 1, 0:ROWS, 0:LANES]
        material2[1, z] = inner2.u[z + 1, 0:ROWS, 0:LANES]
        material2[2, z] = inner2.d[z, 0:ROWS, 0:LANES]

    loop(level2.depth, own_material2)
    ex["mat2"].begin(material2)
    level0.build()
    level1.build()

    fine_w = cheb_weights(2, 0.3, 2.0)
    coarse_w = cheb_weights(4, 0.1, 2.0)

    def cycle(r, out, turn_no):
        level0.start(xa, r, fine_w[0])
        level0.smooth(xb, xa, r, fine_w[1])

        def down0(z):
            sums = level0.defect_sums(xb, r, z)
            scale = fine_w[0] * level1.inv[z]
            for item in range(2):
                r1[item, z + 1] = sums[item]
                ya[item, z + 1] = sums[item] * scale

        loop(level1.depth, down0)
        level1.smooth(yb, ya, r1, fine_w[1])
        own2 = r2_own[turn_no]

        def down1(z):
            sums = level1.defect_sums(yb, r1, z)
            for item in range(2):
                own2[item, z] = sums[item][0:ROWS, 0:LANES]

        loop(level2.depth, down1)
        e2 = ex[("e2a", "e2b")[turn_no]]
        e2.begin(own2)
        own1 = y_own[turn_no]

        def keep(z):
            own1[:, z] = yb[:, z + 1, 0:ROWS, 0:LANES]

        loop(level1.depth, keep)
        e1 = ex[("ya", "yb")[turn_no]]
        e1.begin(own1)
        if turn_no == 0:
            ex["mat2"].finish(material2)
            ex["mat2"].unpack((level2.w, level2.u, level2.k), material2, 3)
            level2.build(True)
        e2.finish(own2)
        e2.unpack(r2, own2, 2)
        level2.start(za, r2, coarse_w[0])
        level2.smooth(zb, za, r2, coarse_w[1])
        level2.smooth(za, zb, r2, coarse_w[2])
        level2.smooth(zb, za, r2, coarse_w[3])
        e1.finish(own1)
        e1.unpack(yb, None, 2)

        def up1(z):
            add = jnp.concatenate([zb[:, z + 1, 0:24], zb[:, z + 1, 40:48]], axis=1)
            ya[:, 2 * z + 1] = yb[:, 2 * z + 1] + add
            ya[:, 2 * z + 2] = yb[:, 2 * z + 2] + add

        loop(level2.depth, up1)
        level1.smooth(yb, ya, r1, fine_w[0])
        level1.smooth(ya, yb, r1, fine_w[1], own_only=True)
        own = x_own[turn_no]

        def up0(z):
            add = ya[:, z + 1, 0:ROWS, 0:LANES]
            own[:, 2 * z] = xb[:, 2 * z + 1, 0:ROWS, 0:LANES] + add
            own[:, 2 * z + 1] = xb[:, 2 * z + 2, 0:ROWS, 0:LANES] + add

        loop(level1.depth, up0)
        e4 = ex[("e4a", "e4b")[turn_no]]
        e4.begin(own)
        e4.finish(own)
        e4.unpack(xa, own, 2)
        level0.smooth(xb, xa, r, fine_w[0])
        level0.smooth(out, xb, r, fine_w[1])

    cycle(r_first, r_second, 0)
    cycle(r_second, r_first, 1)

    def first_image(pair):
        images = level0.operators(r_first, 2 * pair, 2)
        for i in range(2):
            for item in range(2):
                xb[item, 2 * pair + i + 1] = images[i][item]

    loop(depth // 2, first_image)

    def second_image(pair, sums):
        rz, curve = sums
        images = level0.operators(xb, 2 * pair, 2)
        for i in range(2):
            z = 2 * pair + i
            image = jnp.stack([images[i][0][0:ROWS, 0:LANES], images[i][1][0:ROWS, 0:LANES]])
            direction = r_first[:, z + 1, 0:ROWS, 0:LANES]
            direction_out[:, z] = direction
            image_out[:, z] = image
            rz = rz + right_side[:, z] * direction
            curve = curve + direction * image
        return rz, curve

    zero = jnp.zeros((2, ROWS, LANES), jnp.float32)
    rz, curve = lax.fori_loop(0, depth // 2, second_image, (zero, zero))
    part_x[0:2] = rz[:, 0:8] + rz[:, 8:16]
    part_x[2:4] = curve[:, 0:8] + curve[:, 8:16]
    part_y[...] = sum_over("gx", part_x, slots_x, sx_send, sx_recv)
    total = sum_over("gy", part_y, slots_y, sy_send, sy_recv)
    total = jnp.sum(total, axis=2, keepdims=True)
    total = jnp.sum(total, axis=1, keepdims=True)
    alpha_out[...] = jnp.broadcast_to(total[0:2] / total[2:4], alpha_out.shape)


def shards(right_side, classes, sea_mask, kappa_table, cross_table, vertical_table):
    nx, ny = lax.axis_size("gx"), lax.axis_size("gy")
    depth = classes.shape[0]

    def buf(*shape):
        return pltpu.VMEM(shape, jnp.float32)

    def level(size, rows):
        pad, one, face = buf(size + 2, rows, WIDE), buf(size, rows, WIDE), buf(size + 1, rows, WIDE)
        return [pad, pad, pad, one, one, one, one, face, one, one]

    def box(items, size, width):
        sides = buf(items, ROWS + 2 * width, LANES)
        pack = buf(items, ROWS, LANES)
        return [pack, pack, buf(items, size, 2 * width, LANES), sides, sides]

    d0, d1, d2 = depth, depth // 2, depth // 4
    scratch = level(d0, 32) + level(d1, 32) + level(d2, 48) + level(d2, 32)
    scratch += [buf(2, d0 + 2, 32, WIDE)] * 4
    scratch += [buf(2, d1 + 2, 32, WIDE)] * 3
    scratch += [buf(2, d2 + 2, 48, WIDE)] * 3
    scratch += [buf(3, d0, ROWS, LANES), buf(3, d2, ROWS, LANES)]
    scratch += [buf(2, d2, ROWS, LANES)] * 2 + [buf(2, d1, ROWS, LANES)] * 2 + [buf(2, d0, ROWS, LANES)] * 2
    scratch += box(2, d0, 8) + box(3, d0, 8) + box(3, d2, 16) + box(2, d2, 16) + box(2, d2, 16)
    scratch += box(2, d1, 8) + box(2, d1, 8) + box(2, d0, 8) + box(2, d0, 8)
    scratch += [buf(4, 8, LANES)] * 2 + [buf(nx - 1, 4, 8, LANES), buf(ny - 1, 4, 8, LANES)]
    dma = pltpu.SemaphoreType.DMA
    scratch += [dma((9, 8)), dma((9, 8)), dma((nx - 1,)), dma((nx - 1,)), dma((ny - 1,)), dma((ny - 1,))]
    vmem = pl.BlockSpec(memory_space=pltpu.VMEM)
    smem = pl.BlockSpec(memory_space=pltpu.SMEM)
    field = jax.ShapeDtypeStruct(right_side.shape, jnp.float32)
    direction, image, alpha = pl.pallas_call(
        functools.partial(kernel, depth, kappa_table.shape[0]),
        out_shape=(field, field, jax.ShapeDtypeStruct((2, 8, LANES), jnp.float32)),
        in_specs=[vmem, vmem, vmem, smem, smem, smem],
        out_specs=(vmem, vmem, vmem),
        scratch_shapes=scratch,
        compiler_params=pltpu.CompilerParams(
            collective_id=0, has_side_effects=True, vmem_limit_bytes=48 * 1024 * 1024
        ),
    )(right_side, classes, sea_mask, kappa_table, cross_table, vertical_table)
    alpha = alpha[:, 0:1, 0:1, None]
    return alpha * direction, right_side - alpha * image


def solution(mesh):
    return jax.shard_map(
        shards,
        mesh=mesh,
        in_specs=(
            P(None, None, "gx", "gy"),
            P(None, "gx", "gy"),
            P(None, "gx", "gy"),
            P(),
            P(),
            P(),
        ),
        out_specs=(P(None, None, "gx", "gy"), P(None, None, "gx", "gy")),
        check_vma=False,
    )
```

```python
import functools
import math

import jax
import jax.numpy as jnp
from jax import lax
from jax.experimental import pallas as pl
from jax.experimental.pallas import tpu as pltpu
from jax.sharding import PartitionSpec as P

MESH = pl.DeviceIdType.MESH
ROWS, LANES = 16, 128
WIDE = 2 * LANES
WAYS = ((-1, 0), (1, 0), (0, -1), (0, 1), (-1, -1), (1, -1), (-1, 1), (1, 1))


def cheb_weights(degree, lower_end, upper_end):
    middle = 0.5 * (upper_end + lower_end)
    radius = 0.5 * (upper_end - lower_end)
    return [
        1.0 / (middle + radius * math.cos(math.pi * (2 * index_k + 1) / (2 * degree)))
        for index_k in range(degree)
    ]


def turn(value, shift, axis):
    size = value.shape[axis]
    shift = shift % size
    return value if shift == 0 else pltpu.roll(value, shift, axis)


def pair_sum(value, step):
    for axis in (value.ndim - 2, value.ndim - 1):
        place = lax.broadcasted_iota(jnp.int32, value.shape, axis)
        first = (place // step) % 2 == 0
        value = value + jnp.where(first, turn(value, -step, axis), turn(value, step, axis))
    return value


def loop(count, body):
    def run(index, carry):
        body(index)
        return carry

    lax.fori_loop(0, count, run, 0)


class Level:
    def __init__(self, refs, depth, step, factor):
        self.w, self.u, self.k, self.fxm, self.fxp, self.fym, self.fyp, self.fz, self.d, self.inv = refs
        self.depth, self.step, self.factor = depth, step, factor

    def build(self, diagonal_known=False):
        step, factor = self.step, self.factor

        def body(pair):
            stores = []
            for z in (2 * pair, 2 * pair + 1):
                w = self.w[z + 1]
                fxp = factor * jnp.sqrt(w * turn(w, -step, 0))
                fyp = factor * jnp.sqrt(w * turn(w, -step, 1))
                fxm = turn(fxp, step, 0)
                fym = turn(fyp, step, 1)
                fzm = factor * jnp.sqrt(self.u[z] * self.u[z + 1])
                fzp = factor * jnp.sqrt(self.u[z + 1] * self.u[z + 2])
                d = self.k[z + 1]
                if not diagonal_known:
                    d = d + fxm + fxp + fym + fyp + fzm + fzp
                inv = jnp.where(d > 0.0, 1.0 / jnp.where(d > 0.0, d, 1.0), 0.0)
                stores += [(self.fxm, z, fxm), (self.fxp, z, fxp), (self.fym, z, fym), (self.fyp, z, fyp)]
                stores += [(self.fz, z, fzm), (self.fz, z + 1, fzp), (self.d, z, d), (self.inv, z, inv)]
            for ref, z, value in stores:
                ref[z] = value

        loop(self.depth // 2, body)

    def operators(self, v, z, count):
        step = self.step
        images = [[None, None] for _ in range(count)]
        faces = [self.fz[z + i] for i in range(count + 1)]
        for item in range(2):
            planes = [v[item, z + i] for i in range(count + 2)]
            for i in range(count):
                x = planes[i + 1]
                total = self.fxm[z + i] * turn(x, step, 0) + self.fxp[z + i] * turn(x, -step, 0)
                total = total + self.fym[z + i] * turn(x, step, 1) + self.fyp[z + i] * turn(x, -step, 1)
                total = total + faces[i] * planes[i] + faces[i + 1] * planes[i + 2]
                images[i][item] = self.d[z + i] * x - total
        return images

    def start(self, out, r, weight):
        def body(group):
            z = 4 * group
            scale = weight * self.inv[pl.ds(z, 4)]
            out[:, pl.ds(z + 1, 4)] = r[:, pl.ds(z + 1, 4)] * scale

        loop(self.depth // 4, body)

    def smooth(self, out, v, r, weight, own_only=False):
        def body(group):
            z = 4 * group
            images = self.operators(v, z, 4)
            fresh = []
            for i in range(4):
                scale = weight * self.inv[z + i]
                for item in range(2):
                    defect = r[item, z + i + 1] - images[i][item]
                    fresh.append((item, i, v[item, z + i + 1] + scale * defect))
            for item, i, value in fresh:
                if own_only:
                    out[item, z + i + 1, 0:ROWS, 0:LANES] = value[0:ROWS, 0:LANES]
                else:
                    out[item, z + i + 1] = value

        loop(self.depth // 4, body)

    def defect_sums(self, v, r, pair):
        z = 2 * pair
        images = self.operators(v, z, 2)
        sums = []
        for item in range(2):
            q = (r[item, z + 1] - images[0][item]) + (r[item, z + 2] - images[1][item])
            sums.append(pair_sum(q, self.step))
        return sums


class Exchange:
    def __init__(self, refs, send_sem, recv_sem, row, width, depth):
        self.left, self.right, self.rows_in, self.from_right, self.from_left = refs
        self.send_sem, self.recv_sem, self.row = send_sem, recv_sem, row
        self.width, self.depth = width, depth

    def clear(self):
        for ref in (self.rows_in, self.from_right, self.from_left):
            ref[...] = jnp.zeros(ref.shape, jnp.float32)

    def pack(self, source):
        width, groups = self.width, LANES // self.width
        shape = self.left.shape
        group = lax.broadcasted_iota(jnp.int32, shape, 2) // width
        left = jnp.zeros(shape, jnp.float32)
        right = jnp.zeros(shape, jnp.float32)
        for z in range(self.depth):
            moved = turn(source[:, z], width * z, 2)
            left = jnp.where(group == z, moved, left)
            right = jnp.where(group == (z - 1) % groups, moved, right)
        self.left[...] = left
        self.right[...] = right

    def copies(self, source):
        h = self.width
        low, high = pl.ds(0, h), pl.ds(ROWS - h, h)
        near, far = pl.ds(ROWS, h), pl.ds(ROWS + h, h)
        whole = pl.ds(0, ROWS)
        ends = (
            (source.at[:, :, low], self.rows_in.at[:, :, pl.ds(0, h)]),
            (source.at[:, :, high], self.rows_in.at[:, :, pl.ds(h, h)]),
            (self.left, self.from_right.at[:, whole]),
            (self.right, self.from_left.at[:, whole]),
            (self.left.at[:, low], self.from_right.at[:, near]),
            (self.left.at[:, high], self.from_right.at[:, far]),
            (self.right.at[:, low], self.from_left.at[:, near]),
            (self.right.at[:, high], self.from_left.at[:, far]),
        )
        gx, gy = lax.axis_index("gx"), lax.axis_index("gy")
        nx, ny = lax.axis_size("gx"), lax.axis_size("gy")
        for way, ((dx, dy), (src, dst)) in enumerate(zip(WAYS, ends)):
            copy = pltpu.make_async_remote_copy(
                src_ref=src,
                dst_ref=dst,
                send_sem=self.send_sem.at[self.row, way],
                recv_sem=self.recv_sem.at[self.row, way],
                device_id=(lax.rem(gx + dx + nx, nx), lax.rem(gy + dy + ny, ny)),
                device_id_type=MESH,
            )
            yield copy, exists(gx, nx, dx) & exists(gy, ny, dy), exists(gx, nx, -dx) & exists(gy, ny, -dy)

    def begin(self, source):
        self.pack(source)
        for copy, sends, _ in self.copies(source):
            pl.when(sends)(copy.start)

    def finish(self, source):
        for copy, sends, receives in self.copies(source):
            pl.when(sends)(copy.wait_send)
            pl.when(receives)(copy.wait_recv)

    def unpack(self, out, source, count):
        h = self.width
        lane = lax.broadcasted_iota(jnp.int32, self.from_right.shape, 2)
        from_right, from_left = self.from_right[...], self.from_left[...]
        for z in range(self.depth):
            side = jnp.where(
                lane < h,
                turn(from_right, -h * z, 2),
                jnp.where(lane >= LANES - h, turn(from_left, -h * z, 2), 0.0),
            )
            for item in range(count):
                target = out[item] if isinstance(out, tuple) else out.at[item]
                if source is not None:
                    target[z + 1, 0:ROWS, 0:LANES] = source[item, z]
                target[z + 1, ROWS : ROWS + 2 * h, 0:LANES] = self.rows_in[item, z]
                target[z + 1, :, LANES:WIDE] = side[item]


def exists(index, count, step):
    if step < 0:
        return index > 0
    if step > 0:
        return index < count - 1
    return index >= 0


def greet():
    gx, gy = lax.axis_index("gx"), lax.axis_index("gy")
    nx, ny = lax.axis_size("gx"), lax.axis_size("gy")
    barrier = pltpu.get_barrier_semaphore()
    for step in range(1, nx):
        pl.semaphore_signal(barrier, inc=1, device_id=(lax.rem(gx + step, nx), gy), device_id_type=MESH)
    for step in range(1, ny):
        pl.semaphore_signal(barrier, inc=1, device_id=(gx, lax.rem(gy + step, ny)), device_id_type=MESH)
    for dx, dy in WAYS[4:]:
        there = (lax.rem(gx + dx + nx, nx), lax.rem(gy + dy + ny, ny))

        @pl.when(exists(gx, nx, dx) & exists(gy, ny, dy))
        def _():
            pl.semaphore_signal(barrier, inc=1, device_id=there, device_id_type=MESH)

    beside_x = (gx > 0).astype(jnp.int32) + (gx < nx - 1).astype(jnp.int32)
    beside_y = (gy > 0).astype(jnp.int32) + (gy < ny - 1).astype(jnp.int32)
    pl.semaphore_wait(barrier, nx - 1 + ny - 1 + beside_x * beside_y)


def sum_over(axis, mine, slots, send_sem, recv_sem):
    count = lax.axis_size(axis)
    me = lax.axis_index(axis)
    copies = []
    for step in range(1, count):
        copy = pltpu.make_async_remote_copy(
            src_ref=mine,
            dst_ref=slots.at[step - 1],
            send_sem=send_sem.at[step - 1],
            recv_sem=recv_sem.at[step - 1],
            device_id={axis: lax.rem(me + step, count)},
            device_id_type=MESH,
        )
        copy.start()
        copies.append(copy)
    total = mine[...]
    for step, copy in enumerate(copies):
        copy.wait()
        total = total + slots[step]
    return total


def kernel(depth, entries, *refs):
    refs = list(refs)

    def take(count):
        got = tuple(refs[:count])
        del refs[:count]
        return got

    right_side, classes, sea_mask, kappa, cross, vertical = take(6)
    direction_out, image_out, alpha_out = take(3)
    level0 = Level(take(10), depth, 1, 1.0)
    level1 = Level(take(10), depth // 2, 2, 4.0)
    level2 = Level(take(10), depth // 4, 4, 4.0)
    inner2 = Level(take(10), depth // 4, 4, 4.0)
    r_first, r_second, xa, xb = take(4)
    r1, ya, yb = take(3)
    r2, za, zb = take(3)
    material, material2, = take(2)
    r2_own = take(2)
    y_own = take(2)
    x_own = take(2)
    names = ("r", "mat", "mat2", "e2a", "e2b", "ya", "yb", "e4a", "e4b")
    boxes = [take(5) for _ in names]
    part_x, part_y, slots_x, slots_y = take(4)
    send_sem, recv_sem, sx_send, sx_recv, sy_send, sy_recv = take(6)
    widths = (8, 8, 16, 16, 16, 8, 8, 8, 8)
    depths = (depth, depth, depth // 4, depth // 4, depth // 4, depth // 2, depth // 2, depth, depth)
    ex = {
        name: Exchange(box, send_sem, recv_sem, row, width, size)
        for row, (name, box, width, size) in enumerate(zip(names, boxes, widths, depths))
    }
    for exchange in ex.values():
        exchange.clear()
    greet()

    ex["r"].begin(right_side)

    def look_up(group):
        four = pl.ds(4 * group, 4)
        cls = classes[four]
        sea = sea_mask[four].astype(jnp.float32)
        w = jnp.zeros(cls.shape, jnp.float32)
        u, k = w, w
        for entry in range(entries):
            here = cls == entry
            w = jnp.where(here, cross[entry], w)
            u = jnp.where(here, vertical[entry], u)
            k = jnp.where(here, kappa[entry], k)
        material[0, four] = w * sea
        material[1, four] = u * sea
        material[2, four] = k * sea + (1.0 - sea)

    loop(depth // 4, look_up)
    ex["mat"].begin(material)
    for ref in (r_first, r_second, xa, xb, r1, ya, yb, r2, za, zb):
        last = ref.shape[1] - 1
        ref[:, 0] = jnp.zeros(ref.shape[:1] + ref.shape[2:], jnp.float32)
        ref[:, last] = jnp.zeros(ref.shape[:1] + ref.shape[2:], jnp.float32)
    for level in (level0, level1, level2, inner2):
        level.u[0] = jnp.zeros(level.u.shape[1:], jnp.float32)
        level.u[level.depth + 1] = jnp.zeros(level.u.shape[1:], jnp.float32)
    ex["r"].finish(right_side)
    ex["r"].unpack(r_first, right_side, 2)
    ex["mat"].finish(material)
    ex["mat"].unpack((level0.w, level0.u, level0.k), material, 3)

    def coarsen_material(fine, coarse, step):
        def body(z):
            means = []
            for src, factor in ((fine.w, 0.125), (fine.u, 0.125), (fine.k, 1.0)):
                means.append(factor * pair_sum(src[2 * z + 1] + src[2 * z + 2], step))
            for dst, value in zip((coarse.w, coarse.u, coarse.k), means):
                dst[z + 1] = value

        loop(coarse.depth, body)

    coarsen_material(level0, level1, 1)
    coarsen_material(level1, inner2, 2)
    inner2.build()

    def own_material2(z):
        material2[0, z] = inner2.w[z + 1, 0:ROWS, 0:LANES]
        material2[1, z] = inner2.u[z + 1, 0:ROWS, 0:LANES]
        material2[2, z] = inner2.d[z, 0:ROWS, 0:LANES]

    loop(level2.depth, own_material2)
    ex["mat2"].begin(material2)
    level0.build()
    level1.build()

    fine_w = cheb_weights(2, 0.3, 2.0)
    coarse_w = cheb_weights(4, 0.1, 2.0)

    def cycle(r, out, turn_no):
        level0.start(xa, r, fine_w[0])
        level0.smooth(xb, xa, r, fine_w[1])

        def down0(z):
            sums = level0.defect_sums(xb, r, z)
            scale = fine_w[0] * level1.inv[z]
            for item in range(2):
                r1[item, z + 1] = sums[item]
                ya[item, z + 1] = sums[item] * scale

        loop(level1.depth, down0)
        level1.smooth(yb, ya, r1, fine_w[1])
        own2 = r2_own[turn_no]

        def down1(z):
            sums = level1.defect_sums(yb, r1, z)
            for item in range(2):
                own2[item, z] = sums[item][0:ROWS, 0:LANES]

        loop(level2.depth, down1)
        e2 = ex[("e2a", "e2b")[turn_no]]
        e2.begin(own2)
        own1 = y_own[turn_no]

        def keep(z):
            own1[:, z] = yb[:, z + 1, 0:ROWS, 0:LANES]

        loop(level1.depth, keep)
        e1 = ex[("ya", "yb")[turn_no]]
        e1.begin(own1)
        if turn_no == 0:
            ex["mat2"].finish(material2)
            ex["mat2"].unpack((level2.w, level2.u, level2.k), material2, 3)
            level2.build(True)
        e2.finish(own2)
        e2.unpack(r2, own2, 2)
        level2.start(za, r2, coarse_w[0])
        level2.smooth(zb, za, r2, coarse_w[1])
        level2.smooth(za, zb, r2, coarse_w[2])
        level2.smooth(zb, za, r2, coarse_w[3])
        e1.finish(own1)
        e1.unpack(yb, None, 2)

        def up1(z):
            add = jnp.concatenate([zb[:, z + 1, 0:24], zb[:, z + 1, 40:48]], axis=1)
            ya[:, 2 * z + 1] = yb[:, 2 * z + 1] + add
            ya[:, 2 * z + 2] = yb[:, 2 * z + 2] + add

        loop(level2.depth, up1)
        level1.smooth(yb, ya, r1, fine_w[0])
        level1.smooth(ya, yb, r1, fine_w[1], own_only=True)
        own = x_own[turn_no]

        def up0(z):
            add = ya[:, z + 1, 0:ROWS, 0:LANES]
            own[:, 2 * z] = xb[:, 2 * z + 1, 0:ROWS, 0:LANES] + add
            own[:, 2 * z + 1] = xb[:, 2 * z + 2, 0:ROWS, 0:LANES] + add

        loop(level1.depth, up0)
        e4 = ex[("e4a", "e4b")[turn_no]]
        e4.begin(own)
        e4.finish(own)
        e4.unpack(xa, own, 2)
        level0.smooth(xb, xa, r, fine_w[0])
        level0.smooth(out, xb, r, fine_w[1])

    cycle(r_first, r_second, 0)
    cycle(r_second, r_first, 1)

    def first_image(pair):
        images = level0.operators(r_first, 2 * pair, 2)
        for i in range(2):
            for item in range(2):
                xb[item, 2 * pair + i + 1] = images[i][item]

    loop(depth // 2, first_image)

    def second_image(pair, sums):
        rz, curve = sums
        images = level0.operators(xb, 2 * pair, 2)
        for i in range(2):
            z = 2 * pair + i
            image = jnp.stack([images[i][0][0:ROWS, 0:LANES], images[i][1][0:ROWS, 0:LANES]])
            direction = r_first[:, z + 1, 0:ROWS, 0:LANES]
            direction_out[:, z] = direction
            image_out[:, z] = image
            rz = rz + right_side[:, z] * direction
            curve = curve + direction * image
        return rz, curve

    zero = jnp.zeros((2, ROWS, LANES), jnp.float32)
    rz, curve = lax.fori_loop(0, depth // 2, second_image, (zero, zero))
    part_x[0:2] = rz[:, 0:8] + rz[:, 8:16]
    part_x[2:4] = curve[:, 0:8] + curve[:, 8:16]
    part_y[...] = sum_over("gx", part_x, slots_x, sx_send, sx_recv)
    total = sum_over("gy", part_y, slots_y, sy_send, sy_recv)
    total = jnp.sum(total, axis=2, keepdims=True)
    total = jnp.sum(total, axis=1, keepdims=True)
    alpha_out[...] = jnp.broadcast_to(total[0:2] / total[2:4], alpha_out.shape)


def shards(right_side, classes, sea_mask, kappa_table, cross_table, vertical_table):
    nx, ny = lax.axis_size("gx"), lax.axis_size("gy")
    depth = classes.shape[0]

    def buf(*shape):
        return pltpu.VMEM(shape, jnp.float32)

    def level(size, rows):
        pad, one, face = buf(size + 2, rows, WIDE), buf(size, rows, WIDE), buf(size + 1, rows, WIDE)
        return [pad, pad, pad, one, one, one, one, face, one, one]

    def box(items, size, width):
        sides = buf(items, ROWS + 2 * width, LANES)
        pack = buf(items, ROWS, LANES)
        return [pack, pack, buf(items, size, 2 * width, LANES), sides, sides]

    d0, d1, d2 = depth, depth // 2, depth // 4
    scratch = level(d0, 32) + level(d1, 32) + level(d2, 48) + level(d2, 32)
    scratch += [buf(2, d0 + 2, 32, WIDE)] * 4
    scratch += [buf(2, d1 + 2, 32, WIDE)] * 3
    scratch += [buf(2, d2 + 2, 48, WIDE)] * 3
    scratch += [buf(3, d0, ROWS, LANES), buf(3, d2, ROWS, LANES)]
    scratch += [buf(2, d2, ROWS, LANES)] * 2 + [buf(2, d1, ROWS, LANES)] * 2 + [buf(2, d0, ROWS, LANES)] * 2
    scratch += box(2, d0, 8) + box(3, d0, 8) + box(3, d2, 16) + box(2, d2, 16) + box(2, d2, 16)
    scratch += box(2, d1, 8) + box(2, d1, 8) + box(2, d0, 8) + box(2, d0, 8)
    scratch += [buf(4, 8, LANES)] * 2 + [buf(nx - 1, 4, 8, LANES), buf(ny - 1, 4, 8, LANES)]
    dma = pltpu.SemaphoreType.DMA
    scratch += [dma((9, 8)), dma((9, 8)), dma((nx - 1,)), dma((nx - 1,)), dma((ny - 1,)), dma((ny - 1,))]
    vmem = pl.BlockSpec(memory_space=pltpu.VMEM)
    smem = pl.BlockSpec(memory_space=pltpu.SMEM)
    field = jax.ShapeDtypeStruct(right_side.shape, jnp.float32)
    direction, image, alpha = pl.pallas_call(
        functools.partial(kernel, depth, kappa_table.shape[0]),
        out_shape=(field, field, jax.ShapeDtypeStruct((2, 8, LANES), jnp.float32)),
        in_specs=[vmem, vmem, vmem, smem, smem, smem],
        out_specs=(vmem, vmem, vmem),
        scratch_shapes=scratch,
        compiler_params=pltpu.CompilerParams(
            collective_id=0, has_side_effects=True, vmem_limit_bytes=48 * 1024 * 1024
        ),
    )(right_side, classes, sea_mask, kappa_table, cross_table, vertical_table)
    alpha = alpha[:, 0:1, 0:1, None]
    return alpha * direction, right_side - alpha * image


def solution(mesh):
    return jax.shard_map(
        shards,
        mesh=mesh,
        in_specs=(
            P(None, None, "gx", "gy"),
            P(None, "gx", "gy"),
            P(None, "gx", "gy"),
            P(),
            P(),
            P(),
        ),
        out_specs=(P(None, None, "gx", "gy"), P(None, None, "gx", "gy")),
        check_vma=False,
    )
```
